1024 devices in a mesh: dp: 64 (over z, core), tensor: 16 (over y, x).
Axes of the slice: x: 4, y: 4, z: 32, core: 2. Of those that a mesh axis runs over, the one named last changes fastest.
Arguments:
- acts: bfloat16 [16384, 4096], P(('dp', 'tensor')), may hold values from -6 to 6
- out_grad: bfloat16 [16384, 16384], P('dp', 'tensor'), may hold values from -0.375 to 0.375
- q_prev: bfloat16 [64, 16384], P(None, 'tensor'), may hold values from -0.046875 to 0.046875
Outputs:
- basis: float32 [64, 4096], replicated
- factor: float32 [64, 16384], P(None, 'tensor')
The draws below stay inside these ranges and needn't reach their ends.
All inputs are finite; a program needn't handle non-finite values.
Results may differ from the reference program's by a relative error of at most 0.0041.
Values may be sent and summed in bfloat16 or wider, within the bound.
A program may use at most 32 MiB of HBM per device.

```python
import jax
import jax.numpy as jnp
from jax import lax

ROWS = 4096
RANK = 64
TOK = 256
FF = 16384
TOKENS = 16384
N_DP = 64


def shard_levels(rng, dims, shards, low, top_value):
    gain, own = 1.0, jax.random.fold_in(rng, 6)
    for axis_at, parts in shards:
        steps = jnp.exp(jax.random.uniform(jax.random.fold_in(own, axis_at), (parts,), jnp.float32, low / len(shards), top_value / len(shards)))
        gain = gain * jnp.repeat(steps, dims[axis_at] // parts).reshape([-1 if axis == axis_at else 1 for axis in range(len(dims))])
    return gain


def centred(key, extent, deviation, most, shards=(), kind=jnp.bfloat16):
    factor_of = shard_levels(key, extent, shards, -0.22, 0.18) if shards else 1.0
    values = jax.random.normal(key, extent, jnp.float32) * deviation * factor_of
    return jnp.minimum(jnp.maximum(values, -most), most).astype(kind)


def setup_inputs(seed: int = 0) -> dict:
    key_list = jax.random.split(jax.random.key(seed), 4)
    acts = centred(key_list[0], (TOKENS, ROWS), 1.0, 6.0, ((0, 1024),))
    out_grad = centred(key_list[1], (TOKENS, FF), TOK ** -0.5, 0.375, ((0, 64), (1, 16)))
    q_prev = centred(key_list[2], (RANK, FF), FF ** -0.5, 0.046875, ((1, 16),))
    return {"acts": acts, "out_grad": out_grad, "q_prev": q_prev}


def reference(acts, out_grad, q_prev):
    inputs = acts.reshape(N_DP, TOK, ROWS)
    outputs = out_grad.reshape(N_DP, TOK, FF)

    def one_grad(items):
        inp, outp = items
        return jnp.dot(inp.T.astype(jnp.float32), outp.astype(jnp.float32), preferred_element_type=jnp.float32).astype(jnp.bfloat16)

    def left_of(items):
        return jnp.dot(q_prev.astype(jnp.float32), one_grad(items).T.astype(jnp.float32), preferred_element_type=jnp.float32)
    left_terms = lax.map(left_of, (inputs, outputs))
    summed = lax.optimization_barrier(jnp.sum(left_terms, axis=0))
    gram = jnp.dot(summed, summed.T, precision=lax.Precision.HIGHEST)
    lower = jnp.linalg.cholesky(gram)
    basis = lax.linalg.triangular_solve(lower, summed, left_side=True, lower=True)
    low = basis.astype(jnp.bfloat16)

    def right_of(items):
        return jnp.dot(low.astype(jnp.float32), one_grad(items).astype(jnp.float32), preferred_element_type=jnp.float32)
    right_terms = lax.map(right_of, (inputs, outputs))
    factor = lax.optimization_barrier(jnp.sum(right_terms, axis=0)) / N_DP
    return (basis, factor)
```

```python
import jax
import jax.numpy as jnp
from jax import lax
from jax.experimental import pallas as pl
from jax.experimental.pallas import tpu as pltpu
from jax.sharding import PartitionSpec as P

MESH = pl.DeviceIdType.MESH
F32, BF16 = jnp.float32, jnp.bfloat16
HIGH = lax.Precision.HIGHEST
NN = (((1,), (0,)), ((), ()))
NT = (((1,), (1,)), ((), ()))

ACTS, A_RS, A_AG, S_RS, S_EX, S_AG, B_RS, B_AG, S_ALL, F_CORE, F_RS, F_AG, F_OUT = range(13)
STAGES = 13

PLANE = sorted(
    [(a, b) for a in range(4) for b in range(4) if a or b],
    key=lambda p: -(min(p[0], 4 - p[0]) + min(p[1], 4 - p[1])),
)


def two_parts(value):
    high = value.astype(BF16)
    low = (value - high.astype(F32)).astype(BF16)
    return jnp.concatenate([high, low], axis=0)


def dot_parts(left, right, dims):
    both = lax.dot_general(two_parts(left), right, dims, preferred_element_type=F32)
    rows = left.shape[0]
    return both[:rows] + both[rows:]


def add_up(ref, count):
    total = ref[0]
    for i in range(1, count):
        total = total + ref[i]
    return total


def inverse_factor(gram):
    n = gram.shape[0]
    row = lax.broadcasted_iota(jnp.int32, (n, 1), 0)
    eye = lax.broadcasted_iota(jnp.int32, (n, n), 0) == lax.broadcasted_iota(jnp.int32, (n, n), 1)
    m = jnp.concatenate([gram, jnp.where(eye, 1.0, 0.0).astype(F32)], axis=1)
    for j in range(n - 1):
        scale = jnp.where(row > j, m[:, j : j + 1] / m[j : j + 1, j : j + 1], 0.0)
        m = m - scale * m[j : j + 1, :]
    pivots = jnp.sum(jnp.where(eye, m[:, :n], 0.0), axis=1, keepdims=True)
    return m[:, n:] * (1.0 / jnp.sqrt(pivots))


def kernel(
    acts, og, q, basis, factor,
    ac, a_part, a_recv, a_tot, a_full,
    s_part, s_recv, s_red, s_b, s_tot, s_full,
    b_part, b_recv, b_tot, b_full, s_all,
    f_part, f_core, f_half, f_recv, f_tot, f_all,
    ssem, rsem,
):
    dp, te = lax.axis_index("dp"), lax.axis_index("tensor")
    z, c = lax.div(dp, 2), lax.rem(dp, 2)
    y, x = lax.div(te, 4), lax.rem(te, 4)
    mate = 2 * z + 1 - c
    group, g = lax.div(dp, 8), lax.rem(dp, 8)
    plane = [lax.rem(y + a, 4) * 4 + lax.rem(x + b, 4) for a, b in PLANE]
    near = [lax.rem(g + j, 8) for j in range(1, 8)]

    def send(src, dst, stage, to):
        pltpu.make_async_remote_copy(
            src_ref=src, dst_ref=dst, send_sem=ssem.at[stage], recv_sem=rsem.at[stage],
            device_id=to, device_id_type=MESH,
        ).start()

    def arrived(ref, stage):
        pltpu.make_async_copy(ref, ref, rsem.at[stage]).wait()

    def sent(ref, stage):
        pltpu.make_async_copy(ref, ref, ssem.at[stage]).wait()

    barrier = pltpu.get_barrier_semaphore()
    for t in plane:
        pl.semaphore_signal(barrier, inc=1, device_id=(dp, t), device_id_type=MESH)

    def greet(j, carry):
        pl.semaphore_signal(barrier, inc=1, device_id=(lax.rem(dp + 2 * j, 64), te), device_id_type=MESH)
        return carry

    lax.fori_loop(1, 32, greet, 0)
    for j in range(4):
        pl.semaphore_signal(barrier, inc=1, device_id=(8 * group + 2 * j + 1 - c, te), device_id_type=MESH)

    def to_tiles(value, part):
        for p in range(16):
            part[p] = value[8 * (p // 2) : 8 * (p // 2) + 8, 128 * (p % 2) : 128 * (p % 2) + 128]

    def from_tiles(full):
        return jnp.concatenate(
            [jnp.concatenate([full[2 * k], full[2 * k + 1]], axis=1) for k in range(8)], axis=0
        )

    def plane_scatter(part, recv, stage):
        for t in plane:
            send(part.at[t], recv.at[te], stage, (dp, t))

    def plane_sum(part, recv, tot, full, stage):
        recv[te] = part[te]
        arrived(recv.at[pl.ds(0, 15)], stage)
        total = add_up(recv, 16)
        tot[...] = total
        full[te] = total
        for t in plane:
            send(tot, full.at[te], stage + 1, (dp, t))

    to_tiles(lax.dot_general(q[...], og[...], NT, preferred_element_type=F32), a_part)
    own_cols = pl.ds(pl.multiple_of(te * 256, 256), 256)
    own_rows = pl.ds(pl.multiple_of(te * 16, 16), 16)
    ac[own_rows, :] = acts[:, own_cols]

    pl.semaphore_wait(barrier, 15 + 31 + 4)

    plane_scatter(a_part, a_recv, A_RS)
    for t in plane:
        send(acts.at[:, pl.ds(pl.multiple_of(t * 256, 256), 256)], ac.at[own_rows, :], ACTS, (dp, t))
    plane_sum(a_part, a_recv, a_tot, a_full, A_RS)
    arrived(ac.at[pl.ds(0, 240), :], ACTS)
    arrived(a_full.at[pl.ds(0, 15)], A_AG)

    left = dot_parts(from_tiles(a_full), ac[...], NN)
    for k in range(8):
        s_part[k] = left[8 * k : 8 * k + 8, :]
    for m in near:
        send(s_part.at[m], s_recv.at[g], S_RS, (8 * group + m, te))
    s_recv[g] = s_part[g]
    arrived(s_recv.at[pl.ds(0, 7)], S_RS)
    s_red[...] = add_up(s_recv, 8)
    for j in (4, 3, 5, 2, 6, 1, 7):
        send(s_red, s_b.at[group], S_EX, (lax.rem(dp + 8 * j, 64), te))
    s_b[group] = s_red[...]
    arrived(s_b.at[pl.ds(0, 7)], S_EX)
    total = add_up(s_b, 8)
    s_tot[...] = total
    s_full[g] = total
    for m in near:
        send(s_tot, s_full.at[g], S_AG, (8 * group + m, te))
    arrived(s_full.at[pl.ds(0, 7)], S_AG)
    summed = jnp.concatenate([s_full[k] for k in range(8)], axis=0)

    to_tiles(dot_parts(summed, ac[...], NT), b_part)
    plane_scatter(b_part, b_recv, B_RS)
    s_all[te] = summed
    plane_sum(b_part, b_recv, b_tot, b_full, B_RS)
    for t in plane:
        send(s_all.at[te], s_all.at[te], S_ALL, (dp, t))
    arrived(b_full.at[pl.ds(0, 15)], B_AG)

    raw = dot_parts(from_tiles(b_full), og[...], NN)
    for p in range(64):
        h, r, k = p // 32, p % 32 // 8, p % 8
        f_part[h, 8 * r + k] = raw[32 * h + 8 * r : 32 * h + 8 * r + 8, 128 * k : 128 * k + 128]
    send(f_part.at[1 - c], f_core, F_CORE, (mate, te))
    arrived(f_core, F_CORE)
    f_half[...] = f_part[c] + f_core[...]

    def ring(i):
        k = lax.div(i + 1, 2)
        return lax.rem(z + 16 + k - 2 * k * (1 - lax.rem(i, 2)), 32)

    def ring_scatter(i, carry):
        to = ring(i)
        send(f_half.at[to], f_recv.at[z], F_RS, (2 * to + c, te))
        return carry

    def ring_gather(i, carry):
        send(f_tot, f_all.at[c, z], F_AG, (2 * ring(i) + c, te))
        return carry

    lax.fori_loop(0, 31, ring_scatter, 0)
    f_recv[z] = f_half[z]
    arrived(f_recv.at[pl.ds(0, 31)], F_RS)
    total = add_up(f_recv, 32)
    f_tot[...] = total
    f_all[c, z] = total
    lax.fori_loop(0, 31, ring_gather, 0)

    arrived(s_all.at[pl.ds(0, 15)], S_ALL)

    def gram_term(t, carry):
        block = s_all[t]
        return carry + lax.dot_general(block, block, NT, precision=HIGH, preferred_element_type=F32)

    inverse = inverse_factor(lax.fori_loop(0, 16, gram_term, jnp.zeros((64, 64), F32)))

    def basis_block(t, carry):
        cols = pl.ds(pl.multiple_of(t * 256, 256), 256)
        basis[:, cols] = lax.dot_general(inverse, s_all[t], NN, precision=HIGH, preferred_element_type=F32)
        return carry

    lax.fori_loop(0, 16, basis_block, 0)

    arrived(f_all.at[c, pl.ds(0, 31)], F_AG)
    send(f_all.at[c], f_all.at[c], F_OUT, (mate, te))
    arrived(f_core, F_OUT)
    mean = inverse * (1.0 / 64)
    for k in range(8):
        tall = jnp.concatenate([f_all[p // 4, 8 * (p % 4) + k] for p in range(8)], axis=0)
        factor[:, 128 * k : 128 * k + 128] = lax.dot_general(
            mean, tall, NN, precision=HIGH, preferred_element_type=F32
        )

    sent(ac.at[pl.ds(0, 240), :], ACTS)
    sent(a_full.at[pl.ds(0, 15)], A_RS)
    sent(a_full.at[pl.ds(0, 15)], A_AG)
    sent(s_full.at[pl.ds(0, 7)], S_RS)
    sent(s_full.at[pl.ds(0, 7)], S_EX)
    sent(s_full.at[pl.ds(0, 7)], S_AG)
    sent(b_full.at[pl.ds(0, 15)], B_RS)
    sent(b_full.at[pl.ds(0, 15)], B_AG)
    sent(s_all.at[pl.ds(0, 15)], S_ALL)
    sent(f_core, F_CORE)
    sent(f_recv.at[pl.ds(0, 31)], F_RS)
    sent(f_recv.at[pl.ds(0, 31)], F_AG)
    sent(f_core, F_OUT)


def shards(acts, out_grad, q_prev):
    vmem = pl.BlockSpec(memory_space=pltpu.VMEM)
    tiles = pltpu.VMEM((16, 8, 128), F32)
    rows = pltpu.VMEM((8, 8, 256), F32)
    one_tile, one_row = pltpu.VMEM((8, 128), F32), pltpu.VMEM((8, 256), F32)
    half = pltpu.VMEM((32, 8, 128), F32)
    return pl.pallas_call(
        kernel,
        out_shape=(jax.ShapeDtypeStruct((64, 4096), F32), jax.ShapeDtypeStruct((64, 1024), F32)),
        in_specs=[vmem] * 3,
        out_specs=(vmem, vmem),
        scratch_shapes=[
            pltpu.VMEM((256, 256), BF16), tiles, tiles, one_tile, tiles,
            rows, rows, one_row, rows, one_row, rows,
            tiles, tiles, one_tile, tiles, pltpu.VMEM((16, 64, 256), F32),
            pltpu.VMEM((2, 32, 8, 128), F32), half, half, half, one_tile, pltpu.VMEM((2, 32, 8, 128), F32),
            pltpu.SemaphoreType.DMA((STAGES,)), pltpu.SemaphoreType.DMA((STAGES,)),
        ],
        compiler_params=pltpu.CompilerParams(
            collective_id=0, has_side_effects=True, vmem_limit_bytes=32 * 1024 * 1024
        ),
        name="powersgd",
    )(acts, out_grad, q_prev)


def solution(mesh):
    in_specs = (P(("dp", "tensor"), None), P("dp", "tensor"), P(None, "tensor"))
    out_specs = (P(), P(None, "tensor"))
    return jax.shard_map(shards, mesh=mesh, in_specs=in_specs, out_specs=out_specs, check_vma=False)
```
